128 devices in a mesh: seq: 32 (over z, x, core), head: 4 (over y).
Axes of the slice: x: 4, y: 4, z: 4, core: 2. Of those that a mesh axis runs over, the one named last changes fastest.
Arguments:
- qkv: bfloat16 [3, 32768, 40, 128], P(None, 'seq', 'head'), may hold values from -200 to 200
- head_type: int32 [40], P('head'), may hold values from 0 to 1, as said below
- out_weight: bfloat16 [40, 128, 5120], P('head'), may hold values from -0.5 to 0.5
Outputs:
- mixed: bfloat16 [32768, 5120], P(('seq', 'head'))
The draws below stay inside these ranges and needn't reach their ends.
Inputs may be any that keep to these rules, and one draw needn't show every extreme that they name: `head_type`: in each block of 10 consecutive heads exactly 5 heads are temporal (1), the others spatial (0).
All inputs are finite; a program needn't handle non-finite values.
Results may differ from the reference program's by a relative error of at most 0.02.
Values may be sent and summed in bfloat16 or wider, within the bound.
A program may use at most 128 MiB of HBM per device.

```python
import jax
import jax.numpy as jnp
from jax import lax

D = 5120
HEADS = 40
HD = 128
FRAME_TOK = 1024
FRAMES = 32
TOKENS = 32768
HEADS_DEV = 10
TEMP_DEV = 5
N_HEAD = 4


def draw_head_type(key, part):
    key = jax.random.fold_in(key, 11)
    scores = jax.random.randint(key, (N_HEAD, HEADS_DEV), 0, 1048576) * HEADS_DEV + jnp.arange(HEADS_DEV, dtype=jnp.int32)[None, :]
    order = jnp.argsort(scores, axis=1, stable=True)
    ranked = jnp.argsort(order, axis=1, stable=True)
    return (ranked < TEMP_DEV).astype(jnp.int32).reshape(HEADS)


def draw_qkv(key, part):
    key = jax.random.fold_in(key, 5)
    normals = jnp.clip(jax.random.normal(key, (3, TOKENS, HEADS, HD), jnp.float32), -6.0, 6.0)
    return normals.astype(jnp.bfloat16)


def levels(rng, shape, shards, least, high):
    gain = 1.0
    for dim, blocks in shards:
        draws = jax.random.uniform(jax.random.fold_in(jax.random.fold_in(rng, 6), dim), (blocks,), jnp.float32, least / len(shards), high / len(shards))
        gain = gain * jnp.repeat(jnp.exp(draws), shape[dim] // blocks).reshape((-1,) + (1,) * (len(shape) - 1 - dim))
    return gain


def noise(own_key, extent, spread, most, cuts=(), held_as=jnp.bfloat16):
    values = spread * jax.random.normal(own_key, extent, jnp.float32)
    if cuts:
        values = values * levels(own_key, extent, cuts, -0.22, 0.18)
    return jnp.clip(values, -most, most).astype(held_as)


def setup_inputs(seed: int = 0) -> dict:
    splits = jax.random.split(jax.random.key(seed), 4)
    qkv = draw_qkv(jax.random.fold_in(splits[3], 71), 0)
    head_type = draw_head_type(jax.random.fold_in(splits[3], 71), 0)
    out_weight = noise(splits[2], (HEADS, HD, D), HD ** -0.5, 0.5, ((0, 4),))
    return dict(qkv=qkv, head_type=head_type, out_weight=out_weight)


def attend(query_matrix, key_matrix, value_matrix, softmax_scale):
    attention_logits = jnp.einsum("gnz,gcz->gnc", query_matrix.astype(jnp.float32), key_matrix.astype(jnp.float32)) * softmax_scale
    highest = jnp.max(attention_logits, axis=-1, keepdims=True)
    weights = jnp.exp(attention_logits - highest)
    summed = jnp.sum(weights, axis=-1, keepdims=True)
    attention_probs = (weights / summed).astype(jnp.bfloat16)
    attended_output = jnp.einsum("clg,cgz->clz", attention_probs.astype(jnp.float32), value_matrix.astype(jnp.float32))
    return attended_output.astype(jnp.bfloat16)


def reference(qkv, head_type, out_weight):
    softmax_scale = HD ** -0.5
    per_head = jnp.moveaxis(qkv, 2, 0)

    def one_head(pair):
        stacked, head_kind = pair

        def spatial_way():
            framed = stacked.reshape(3, FRAMES, FRAME_TOK, HD)
            return attend(framed[0], framed[1], framed[2], softmax_scale).reshape(TOKENS, HD)

        def temporal_way():
            framed = jnp.transpose(stacked.reshape(3, FRAMES, FRAME_TOK, HD), (0, 2, 1, 3))
            attended_output = attend(framed[0], framed[1], framed[2], softmax_scale)
            return jnp.transpose(attended_output, (1, 0, 2)).reshape(TOKENS, HD)

        return lax.cond(head_kind == 1, temporal_way, spatial_way)

    attention = lax.map(one_head, (per_head, head_type))
    summed = jnp.zeros((TOKENS, D), jnp.float32)
    for group in range(N_HEAD):
        block_heads = attention[group * HEADS_DEV:(group + 1) * HEADS_DEV]
        flat = jnp.transpose(block_heads, (1, 0, 2)).reshape(TOKENS, HEADS_DEV * HD)
        weight_rows = out_weight[group * HEADS_DEV:(group + 1) * HEADS_DEV].reshape(HEADS_DEV * HD, D)
        partial_sum = jnp.dot(flat, weight_rows, preferred_element_type=jnp.float32).astype(jnp.bfloat16)
        summed = summed + partial_sum.astype(jnp.float32)
    return summed.astype(jnp.bfloat16)
```

```python
import functools

import jax
import jax.numpy as jnp
from jax import lax
from jax.experimental import pallas as pl
from jax.experimental.pallas import tpu as pltpu
from jax.sharding import PartitionSpec as P

MESH = pl.DeviceIdType.MESH
BLOCK = 16
CHUNKS = 4
NEG = -1e30


def softmax_times(scores, values, factor):
    highest = jnp.max(scores, axis=-1, keepdims=True)
    weights = jnp.exp2((scores - highest) * factor)
    total = jnp.sum(weights, axis=-1, keepdims=True)
    mixed = jnp.dot(weights.astype(jnp.bfloat16), values, preferred_element_type=jnp.float32)
    return (mixed / total).astype(jnp.bfloat16)


def scores_of(queries, keys):
    return lax.dot_general(queries, keys, (((1,), (1,)), ((), ())), preferred_element_type=jnp.float32)


def kernel(
    n_seq, n_head, chunks, kind_ref, qkv_hbm, weight_hbm, out_hbm,
    qkv, weight, packed, arrived, answers, returned, attended, partial, passing, order,
    qkv_sem, weight_sem, there_send, there_recv, back_send, back_recv, ring_send, ring_recv, out_sem,
):
    heads, tokens, width = qkv.shape[1:]
    half = heads // 2
    dests = tokens // BLOCK // chunks
    stride = n_seq // dests
    rows = tokens // n_head // chunks
    per_owner = rows // BLOCK
    share = tokens // n_head
    columns = weight.shape[2] // 2
    factor = width**-0.5 * 1.4426950408889634
    s = lax.axis_index("seq")
    g = lax.axis_index("head")
    right, left = lax.rem(g + 1, n_head), lax.rem(g + n_head - 1, n_head)
    side = (right, left)

    qkv_copy = pltpu.make_async_copy(qkv_hbm, qkv, qkv_sem)
    qkv_copy.start()
    weight_copy = pltpu.make_async_copy(weight_hbm, weight, weight_sem)

    barrier = pltpu.get_barrier_semaphore()

    def greet(i, _):
        pl.semaphore_signal(barrier, inc=1, device_id={"seq": lax.rem(s + i, n_seq), "head": g}, device_id_type=MESH)
        return 0

    lax.fori_loop(1, n_seq, greet, 0)
    for y in side:
        pl.semaphore_signal(barrier, inc=1, device_id={"seq": s, "head": y}, device_id_type=MESH)

    found = [jnp.int32(0), jnp.int32(0)]
    listed = [jnp.int32(0)] * heads
    for i in range(heads):
        temporal = kind_ref[i] == 1
        place = jnp.where(temporal, found[1] + half, found[0])
        for j in range(heads):
            listed[j] = jnp.where(place == j, jnp.int32(i), listed[j])
        found[0] = found[0] + jnp.where(temporal, 0, 1)
        found[1] = found[1] + jnp.where(temporal, 1, 0)
    for j in range(heads):
        order[j] = listed[j]

    qkv_copy.wait()
    weight_copy.start()

    def pack(i, _):
        packed[i] = qkv[i // half, order[half + lax.rem(i, half)]]
        return 0

    lax.fori_loop(0, 3 * half, pack, 0)
    pl.semaphore_wait(barrier, n_seq - 1 + 2)

    def is_dest(c):
        return lax.rem(s, stride) == lax.rem(c, stride)

    def send_there(c):
        slot = c // stride

        def one(i, _):
            j = lax.rem(i + s // stride, dests)
            to = j * stride + lax.rem(c, stride)
            first = pl.multiple_of(share * (j // per_owner) + rows * c + BLOCK * lax.rem(j, per_owner), BLOCK)
            src = packed.at[:, pl.ds(first, BLOCK), :]
            dst = arrived.at[slot, s]

            @pl.when(to == s)
            def _():
                pltpu.make_async_copy(src, dst, there_recv.at[slot]).start()

            @pl.when(to != s)
            def _():
                pltpu.make_async_remote_copy(
                    src_ref=src, dst_ref=dst, send_sem=there_send.at[c], recv_sem=there_recv.at[slot],
                    device_id={"seq": to, "head": g}, device_id_type=MESH,
                ).start()

            return 0

        lax.fori_loop(0, dests, one, 0)

    def temporal_part(c):
        slot = c // stride
        block = s // stride

        @pl.when(is_dest(c))
        def _():
            pltpu.make_async_copy(arrived.at[slot], arrived.at[slot], there_recv.at[slot]).wait()
            n = n_seq * BLOCK
            piece = n // 2
            same = lax.rem(lax.broadcasted_iota(jnp.int32, (piece, n), 0), BLOCK) == lax.rem(
                lax.broadcasted_iota(jnp.int32, (piece, n), 1), BLOCK
            )
            for h in range(half):
                keys = arrived[slot, :, half + h].reshape(n, width)
                values = arrived[slot, :, 2 * half + h].reshape(n, width)
                for p in range(2):
                    of = pl.ds(p * (n_seq // 2), n_seq // 2)
                    queries = arrived[slot, of, h].reshape(piece, width)
                    scores = jnp.where(same, scores_of(queries, keys), NEG)
                    answers[slot, of, h] = softmax_times(scores, values, factor).reshape(n_seq // 2, BLOCK, width)

            def one(i, _):
                to = lax.rem(i + s, n_seq)
                src = answers.at[slot, to]
                dst = returned.at[c, block]

                @pl.when(to == s)
                def _():
                    pltpu.make_async_copy(src, dst, back_recv.at[c]).start()

                @pl.when(to != s)
                def _():
                    pltpu.make_async_remote_copy(
                        src_ref=src, dst_ref=dst, send_sem=back_send.at[slot], recv_sem=back_recv.at[c],
                        device_id={"seq": to, "head": g}, device_id_type=MESH,
                    ).start()

                return 0

            lax.fori_loop(0, n_seq, one, 0)

    def spatial_part(c):
        slot = lax.rem(c, 2)
        for h in range(half):
            head = order[h]
            queries = jnp.concatenate(
                [qkv[0, head, pl.ds(pl.multiple_of(share * o + rows * c, BLOCK), rows), :] for o in range(n_head)], axis=0
            )
            attended[slot, :, h * width : (h + 1) * width] = softmax_times(
                scores_of(queries, qkv[1, head]), qkv[2, head], factor
            )

    def project(c):
        slot = lax.rem(c, 2)
        pltpu.make_async_copy(returned.at[c], returned.at[c], back_recv.at[c]).wait()
        for h in range(half):
            attended[slot, :, (half + h) * width : (half + h + 1) * width] = returned[c, :, h].reshape(
                n_head * rows, width
            )
        tile = 512 if columns % 512 == 0 else columns
        for d in range(2):
            for t in range(columns // tile):
                cols = slice(d * columns + t * tile, d * columns + (t + 1) * tile)
                total = None
                for k in range(half):
                    pair = jnp.concatenate([weight[order[2 * k], :, cols], weight[order[2 * k + 1], :, cols]], axis=0)
                    term = jnp.dot(
                        attended[slot, :, 2 * k * width : 2 * (k + 1) * width], pair, preferred_element_type=jnp.float32
                    )
                    total = term if total is None else total + term
                partial[c, d, :, :, t * tile : (t + 1) * tile] = total.astype(jnp.bfloat16).reshape(n_head, rows, tile)

    def ring_copy(c, d, t):
        if t == 0:
            owner = lax.rem(g + (n_head - 1 if d == 0 else 1), n_head)
            src = partial.at[c, d, owner]
        else:
            src = passing.at[c, d, t - 1]
        return pltpu.make_async_remote_copy(
            src_ref=src, dst_ref=passing.at[c, d, t], send_sem=ring_send.at[c, d, t], recv_sem=ring_recv.at[c, d, t],
            device_id={"seq": s, "head": side[d]}, device_id_type=MESH,
        )

    def add_own(c, d, t):
        owner = lax.rem(g + (2 * n_head - 2 - t if d == 0 else 2 + t), n_head)
        passing[c, d, t] = (passing[c, d, t].astype(jnp.float32) + partial[c, d, owner].astype(jnp.float32)).astype(
            jnp.bfloat16
        )

    def ring_step(c, t):
        for d in range(2):
            ring_copy(c, d, t).wait_recv()
            add_own(c, d, t)
            ring_copy(c, d, t + 1).start()

    def out_copy(c, d):
        return pltpu.make_async_copy(
            passing.at[c, d, n_head - 2],
            out_hbm.at[pl.ds(pl.multiple_of(rows * c, BLOCK), rows), pl.ds(d * columns, columns)],
            out_sem.at[c, d],
        )

    def ring_end(c):
        for d in range(2):
            ring_copy(c, d, n_head - 2).wait_recv()
            add_own(c, d, n_head - 2)
            out_copy(c, d).start()

    def when_in(c, what):
        @pl.when(jnp.logical_and(c >= 0, c < chunks))
        def _():
            what(c)

    send_there(jnp.int32(0))
    send_there(jnp.int32(1))
    spatial_part(jnp.int32(0))
    temporal_part(jnp.int32(0))
    weight_copy.wait()

    def tick(k, _):
        when_in(k - n_head + 1, ring_end)
        for t in range(n_head - 3, -1, -1):
            when_in(k - 1 - t, functools.partial(ring_step, t=t))

        def start(c):
            project(c)
            for d in range(2):
                ring_copy(c, d, 0).start()

        when_in(k + 2, send_there)
        when_in(k + 1, spatial_part)
        when_in(k, start)
        when_in(k + 1, temporal_part)
        return 0

    lax.fori_loop(0, chunks + n_head - 1, tick, 0)

    def finish(c, _):
        for d in range(2):
            for t in range(n_head - 1):
                ring_copy(c, d, t).wait_send()
            out_copy(c, d).wait()

        @pl.when(is_dest(c))
        def _():
            few = packed.at[:, pl.ds(0, BLOCK * (dests - 1)), :]
            pltpu.make_async_copy(few, few, there_send.at[c]).wait()
            slot = c // stride
            most = answers.at[slot, pl.ds(0, n_seq - 1)]
            pltpu.make_async_copy(most, most, back_send.at[slot]).wait()

        @pl.when(jnp.logical_not(is_dest(c)))
        def _():
            all_ = packed.at[:, pl.ds(0, BLOCK * dests), :]
            pltpu.make_async_copy(all_, all_, there_send.at[c]).wait()

        return 0

    lax.fori_loop(0, chunks, finish, 0)


def shards(n_seq, n_head, chunks, qkv, head_type, out_weight):
    kinds, tokens, heads, width = qkv.shape
    model = out_weight.shape[2]
    half = heads // 2
    dests = tokens // BLOCK // chunks
    slots = chunks * dests // n_seq
    rows = tokens // n_head // chunks
    bf16 = jnp.bfloat16
    dma = pltpu.SemaphoreType.DMA
    any_ = pl.BlockSpec(memory_space=pl.ANY)
    return pl.pallas_call(
        functools.partial(kernel, n_seq, n_head, chunks),
        out_shape=jax.ShapeDtypeStruct((tokens // n_head, model), bf16),
        in_specs=[pl.BlockSpec(memory_space=pltpu.SMEM), any_, any_],
        out_specs=any_,
        scratch_shapes=[
            pltpu.VMEM((3, heads, tokens, width), bf16),
            pltpu.VMEM((heads, width, model), bf16),
            pltpu.VMEM((3 * half, tokens, width), bf16),
            pltpu.VMEM((slots, n_seq, 3 * half, BLOCK, width), bf16),
            pltpu.VMEM((slots, n_seq, half, BLOCK, width), bf16),
            pltpu.VMEM((chunks, dests, half, BLOCK, width), bf16),
            pltpu.VMEM((2, n_head * rows, heads * width), bf16),
            pltpu.VMEM((chunks, 2, n_head, rows, model // 2), bf16),
            pltpu.VMEM((chunks, 2, n_head - 1, rows, model // 2), bf16),
            pltpu.SMEM((heads,), jnp.int32),
            dma,
            dma,
            dma((chunks,)),
            dma((slots,)),
            dma((slots,)),
            dma((chunks,)),
            dma((chunks, 2, n_head - 1)),
            dma((chunks, 2, n_head - 1)),
            dma((chunks, 2)),
        ],
        compiler_params=pltpu.CompilerParams(
            collective_id=0, has_side_effects=True, vmem_limit_bytes=62 * 1024 * 1024
        ),
        cost_estimate=pl.CostEstimate(flops=17_000_000_000, bytes_accessed=24_000_000, transcendentals=6_000_000),
    )(head_type, jnp.transpose(qkv, (0, 2, 1, 3)), out_weight)


def solution(mesh):
    n_seq, n_head = mesh.shape["seq"], mesh.shape["head"]
    return jax.shard_map(
        functools.partial(shards, n_seq, n_head, CHUNKS),
        mesh=mesh,
        in_specs=(P(None, "seq", "head", None), P("head"), P("head", None, None)),
        out_specs=P(("seq", "head"), None),
        check_vma=False,
    )
```

```python
import functools
import math

import jax
import jax.numpy as jnp
from jax import lax
from jax.experimental import pallas as pl
from jax.experimental.pallas import tpu as pltpu
from jax.sharding import PartitionSpec as P

MESH = pl.DeviceIdType.MESH
BLOCK = 8
CHUNKS = 8
UNROLL = 1
STREAMS = 2
NEG = -1e30
TICK = (
    ("ring1", 0, 2, 0, 7),
    ("spatial", 0, -1, 0, 7),
    ("ring0", 0, 1, 0, 7),
    ("send", 1, -1, 0, 7),
    ("ring0", 1, 1, 0, 7),
    ("ring2", 1, 4, 0, 7),
    ("temporal", 2, -1, 0, 7),
    ("send", 2, -2, 0, 7),
    ("project", 0, 0, 0, 7),
    ("ring2", 0, 3, 0, 7),
    ("temporal", 0, -1, 0, 7),
    ("project", 1, 0, 0, 7),
    ("temporal", 1, -1, 0, 7),
    ("send", 0, -2, 0, 7),
    ("ring1", 1, 2, 0, 7),
)


def softmax_times(scores, values, factor):
    highest = jnp.max(scores, axis=-1, keepdims=True)
    weights = jnp.exp2((scores - highest) * factor)
    total = jnp.sum(weights, axis=-1, keepdims=True)
    mixed = jnp.dot(weights.astype(jnp.bfloat16), values, preferred_element_type=jnp.float32)
    return mixed / total


def scores_of(queries, keys):
    return lax.dot_general(queries, keys, (((1,), (1,)), ((), ())), preferred_element_type=jnp.float32)


def kernel(
    n_seq, n_head, chunks, kind_ref, qkv_hbm, weight_hbm, out_hbm,
    qkv, weight, packed, arrived, answers, returned, attended, partial, passing, order,
    qkv_sem, weight_sem, there_send, there_recv, back_send, back_recv, ring_send, ring_recv, out_sem,
):
    heads, tokens, width = qkv.shape[1:]
    half = heads // 2
    groups = (half + 1) // 2
    dests = tokens // BLOCK // chunks
    stride = n_seq // dests
    share = tokens // n_head
    rows = share // chunks
    per_owner = rows // BLOCK
    side_columns = weight.shape[2] // 2
    columns = side_columns // STREAMS
    tiles = packed.shape[2]
    factor = width**-0.5 * math.log2(math.e)
    s = lax.axis_index("seq")
    g = lax.axis_index("head")
    side = (lax.rem(g + 1, n_head), lax.rem(g + n_head - 1, n_head))

    def wrapped(i, n):
        return jnp.where(i >= n, i - n, i)

    block = lax.div(s, stride)
    phase = lax.rem(s, stride)

    qkv_copy = pltpu.make_async_copy(qkv_hbm, qkv, qkv_sem)
    weight_copy = pltpu.make_async_copy(weight_hbm, weight, weight_sem)
    qkv_copy.start()

    barrier = pltpu.get_barrier_semaphore()

    def greet(i, _):
        pl.semaphore_signal(barrier, inc=1, device_id={"seq": wrapped(s + i, n_seq), "head": g}, device_id_type=MESH)
        return 0

    lax.fori_loop(1, n_seq, greet, 0)
    for y in side:
        pl.semaphore_signal(barrier, inc=1, device_id={"seq": s, "head": y}, device_id_type=MESH)

    found = [jnp.int32(0), jnp.int32(0)]
    listed = [jnp.int32(0)] * heads
    for i in range(heads):
        temporal = kind_ref[i] == 1
        place = jnp.where(temporal, found[1] + half, found[0])
        for j in range(heads):
            listed[j] = jnp.where(place == j, jnp.int32(i), listed[j])
        found[0] = found[0] + jnp.where(temporal, 0, 1)
        found[1] = found[1] + jnp.where(temporal, 1, 0)
    for j in range(heads):
        order[j] = listed[j]

    def tiles_of(q):
        return pl.ds(3 * q, min(3, tiles - 3 * q))

    def unit(kind, h):
        at = 6 * (h // 2) + 3 * (h % 2) + kind
        return at // 2, at % 2

    def pack(c, q):
        for o in range(n_head):
            of = pl.ds(pl.multiple_of(share * o + rows * c, rows), rows)
            found = {}
            for h in range(2 * q, min(2 * q + 2, half)):
                for kind in range(3):
                    found[unit(kind, h)] = (
                        qkv[kind, order[half + h], of, :].astype(jnp.float32).reshape(per_owner, BLOCK, width)
                    )
            for t in sorted({at[0] for at in found}):
                low = found[t, 0]
                both = jnp.concatenate([low, found.get((t, 1), low)], axis=1)
                packed[c, pl.ds(o * per_owner, per_owner), t] = both.astype(jnp.bfloat16)

    def part_of(tile, upper):
        half_tile = tile.astype(jnp.float32)[:, BLOCK * upper : BLOCK * (upper + 1)]
        return half_tile.reshape(half_tile.shape[0] * BLOCK, width).astype(jnp.bfloat16)

    def is_dest(c):
        return phase == lax.rem(c, stride)

    def send(c, q):
        pack(c, q)
        send_packed(c, q)

    def send_packed(c, q):
        slot = lax.div(c, stride)

        near, dst = lax.rem(c, stride), arrived.at[slot, s, tiles_of(q)]

        def remote(j):
            pltpu.make_async_remote_copy(
                src_ref=packed.at[c, j, tiles_of(q)], dst_ref=dst,
                send_sem=there_send.at[c, q], recv_sem=there_recv.at[slot, q],
                device_id={"seq": j * stride + near, "head": g}, device_id_type=MESH,
            ).start()

        @pl.when(is_dest(c))
        def _():
            pltpu.make_async_copy(packed.at[c, block, tiles_of(q)], dst, there_recv.at[slot, q]).start()

        @pl.when(jnp.logical_not(is_dest(c)))
        def _():
            remote(block)

        def one(i, _):
            remote(wrapped(block + i, dests))
            return 0

        lax.fori_loop(1, dests, one, 0, unroll=UNROLL)

    def temporal(c, q):
        slot = lax.div(c, stride)

        @pl.when(is_dest(c))
        def _():
            whole = arrived.at[slot, :, tiles_of(q)]
            pltpu.make_async_copy(whole, whole, there_recv.at[slot, q]).wait()
            n = n_seq * BLOCK
            same = lax.rem(lax.broadcasted_iota(jnp.int32, (n, n), 0), BLOCK) == lax.rem(
                lax.broadcasted_iota(jnp.int32, (n, n), 1), BLOCK
            )
            done = []
            for h in range(2 * q, min(2 * q + 2, half)):
                queries, keys, values = (
                    part_of(arrived[slot, :, unit(kind, h)[0]], unit(kind, h)[1]) for kind in range(3)
                )
                scores = jnp.where(same, scores_of(queries, keys), NEG)
                done.append(softmax_times(scores, values, factor).reshape(n_seq, BLOCK, width))
            answers[slot, q] = jnp.concatenate([done[0], done[-1]], axis=1).astype(jnp.bfloat16)

            dst = returned.at[c, q, block]
            pltpu.make_async_copy(answers.at[slot, q, s], dst, back_recv.at[c, q]).start()

            def one(i, _):
                to = wrapped(s + i, n_seq)
                pltpu.make_async_remote_copy(
                    src_ref=answers.at[slot, q, to], dst_ref=dst,
                    send_sem=back_send.at[slot, q], recv_sem=back_recv.at[c, q],
                    device_id={"seq": to, "head": g}, device_id_type=MESH,
                ).start()
                return 0

            lax.fori_loop(1, n_seq, one, 0, unroll=UNROLL)

    def spatial(c, _):
        slot = lax.rem(c, 2)
        for h in range(half):
            head = order[h]
            queries = jnp.concatenate(
                [qkv[0, head, pl.ds(pl.multiple_of(share * o + rows * c, rows), rows), :] for o in range(n_head)], axis=0
            )
            attended[slot, :, h * width : (h + 1) * width] = softmax_times(
                scores_of(queries, qkv[1, head]), qkv[2, head], factor
            ).astype(jnp.bfloat16)

    def ring_start(c, d, t, h):
        owner = lax.rem(g + (n_head - 1 if d == 0 else 1), n_head)
        pltpu.make_async_remote_copy(
            src_ref=partial.at[c, d, h, owner] if t == 0 else passing.at[c, d, h, t - 1],
            dst_ref=passing.at[c, d, h, t], send_sem=ring_send.at[c, d, h, t], recv_sem=ring_recv.at[c, d, h, t],
            device_id={"seq": s, "head": side[d]}, device_id_type=MESH,
        ).start()

    def ring_wait(c, d, t, h, sem):
        pltpu.make_async_copy(passing.at[c, d, h, t], passing.at[c, d, h, t], sem.at[c, d, h, t]).wait()

    def project(c, h):
        slot = lax.rem(c, 2)
        if h == 0:
            for q in range(groups):
                pltpu.make_async_copy(returned.at[c, q], returned.at[c, q], back_recv.at[c, q]).wait()
            for i in range(half):
                attended[slot, :, (half + i) * width : (half + i + 1) * width] = part_of(returned[c, i // 2], i % 2)
        step = 256 if columns % 256 == 0 else columns
        for d in range(2):
            for t in range(0, columns, step):
                cols = pl.ds(d * side_columns + h * columns + t, step)
                rows_of = jnp.concatenate([weight[order[i], :, cols] for i in range(heads)], axis=0)
                total = jnp.dot(attended[slot], rows_of, preferred_element_type=jnp.float32)
                partial[c, d, h, :, :, t : t + step] = total.astype(jnp.bfloat16).reshape(n_head, rows, step)
            ring_start(c, d, 0, h)

    def out_copy(c, d, h):
        return pltpu.make_async_copy(
            passing.at[c, d, h, n_head - 2],
            out_hbm.at[pl.ds(pl.multiple_of(rows * c, rows), rows), pl.ds(d * side_columns + h * columns, columns)],
            out_sem.at[c, d, h],
        )

    def ring(t):
        def step(c, h):
            for d in range(2):
                ring_wait(c, d, t, h, ring_recv)
                owner = lax.rem(g + (2 * n_head - 2 - t if d == 0 else 2 + t), n_head)
                total = passing[c, d, h, t].astype(jnp.float32) + partial[c, d, h, owner].astype(jnp.float32)
                passing[c, d, h, t] = total.astype(jnp.bfloat16)
                if t < n_head - 2:
                    ring_start(c, d, t + 1, h)
                else:
                    out_copy(c, d, h).start()

        return step

    does = dict(send=send, temporal=temporal, spatial=spatial, project=project)
    for t in range(n_head - 1):
        does["ring%d" % t] = ring(t)
    lags = [entry[2] for entry in TICK]

    qkv_copy.wait()
    weight_copy.start()
    for q in range(groups):
        pack(jnp.int32(0), q)
    pl.semaphore_wait(barrier, n_seq - 1 + 2)
    for q in range(groups):
        send_packed(jnp.int32(0), q)

    def tick(k, _):
        for what, part, lag, first, last in TICK:
            c = k - lag
            first = 1 if what == "send" and first == 0 else first

            @pl.when(jnp.logical_and(c >= first, c <= last))
            def _(what=what, part=part, c=c):
                does[what](c, part)

        if min(lags) < 0:
            @pl.when(k == -1)
            def _():
                weight_copy.wait()

        return 0

    lax.fori_loop(min(lags), chunks + max(lags), tick, 0)

    def finish(c, _):
        slot = lax.div(c, stride)
        for h in range(STREAMS):
            for d in range(2):
                for t in range(n_head - 1):
                    ring_wait(c, d, t, h, ring_send)
                out_copy(c, d, h).wait()

        @pl.when(is_dest(c))
        def _():
            for q in range(groups):
                few = packed.at[c, pl.ds(0, dests - 1), tiles_of(q)]
                pltpu.make_async_copy(few, few, there_send.at[c, q]).wait()
                most = answers.at[slot, q, pl.ds(0, n_seq - 1)]
                pltpu.make_async_copy(most, most, back_send.at[slot, q]).wait()

        @pl.when(jnp.logical_not(is_dest(c)))
        def _():
            for q in range(groups):
                every = packed.at[c, :, tiles_of(q)]
                pltpu.make_async_copy(every, every, there_send.at[c, q]).wait()

        return 0

    lax.fori_loop(0, chunks, finish, 0)


def shards(n_seq, n_head, chunks, qkv, head_type, out_weight):
    kinds, tokens, heads, width = qkv.shape
    model = out_weight.shape[2]
    half = heads // 2
    groups, tiles = (half + 1) // 2, (3 * half + 1) // 2
    dests = tokens // BLOCK // chunks
    slots = chunks * dests // n_seq
    rows = tokens // n_head // chunks
    part = model // 2 // STREAMS
    bf16 = jnp.bfloat16
    dma = pltpu.SemaphoreType.DMA
    any_ = pl.BlockSpec(memory_space=pl.ANY)
    return pl.pallas_call(
        functools.partial(kernel, n_seq, n_head, chunks),
        out_shape=jax.ShapeDtypeStruct((tokens // n_head, model), bf16),
        in_specs=[pl.BlockSpec(memory_space=pltpu.SMEM), any_, any_],
        out_specs=any_,
        scratch_shapes=[
            pltpu.VMEM((kinds, heads, tokens, width), bf16),
            pltpu.VMEM((heads, width, model), bf16),
            pltpu.VMEM((chunks, dests, tiles, 2 * BLOCK, width), bf16),
            pltpu.VMEM((slots, n_seq, tiles, 2 * BLOCK, width), bf16),
            pltpu.VMEM((slots, groups, n_seq, 2 * BLOCK, width), bf16),
            pltpu.VMEM((chunks, groups, dests, 2 * BLOCK, width), bf16),
            pltpu.VMEM((2, n_head * rows, heads * width), bf16),
            pltpu.VMEM((chunks, 2, STREAMS, n_head, rows, part), bf16),
            pltpu.VMEM((chunks, 2, STREAMS, n_head - 1, rows, part), bf16),
            pltpu.SMEM((heads,), jnp.int32),
            dma,
            dma,
            dma((chunks, groups)),
            dma((slots, groups)),
            dma((slots, groups)),
            dma((chunks, groups)),
            dma((chunks, 2, STREAMS, n_head - 1)),
            dma((chunks, 2, STREAMS, n_head - 1)),
            dma((chunks, 2, STREAMS)),
        ],
        compiler_params=pltpu.CompilerParams(
            collective_id=0, has_side_effects=True, vmem_limit_bytes=62 * 1024 * 1024
        ),
        cost_estimate=pl.CostEstimate(flops=17_000_000_000, bytes_accessed=24_000_000, transcendentals=6_000_000),
    )(head_type, jnp.transpose(qkv, (0, 2, 1, 3)), out_weight)


def solution(mesh):
    n_seq, n_head = mesh.shape["seq"], mesh.shape["head"]
    return jax.shard_map(
        functools.partial(shards, n_seq, n_head, CHUNKS),
        mesh=mesh,
        in_specs=(P(None, "seq", "head", None), P("head"), P("head", None, None)),
        out_specs=P(("seq", "head"), None),
        check_vma=False,
    )
```

```python
import functools
import math

import jax
import jax.numpy as jnp
from jax import lax
from jax.experimental import pallas as pl
from jax.experimental.pallas import tpu as pltpu
from jax.sharding import PartitionSpec as P

MESH = pl.DeviceIdType.MESH
BLOCK = 8
CHUNKS = 8
UNROLL = 1
STREAMS = 2
NEG = -1e30
START = (
    ("send_packed", 2, 0),
    ("send_packed", 0, 0),
    ("send_packed", 1, 0),
    ("temporal", 0, 0),
    ("temporal", 2, 0),
    ("temporal", 1, 0),
    ("send", 2, 1),
    ("send", 1, 1),
    ("spatial", 0, 0),
    ("send", 0, 1),
)
TICK = (
    ("project", 0, 0, 0, 7),
    ("temporal", 2, -1, 1, 7),
    ("project", 1, 0, 0, 7),
    ("ring1", 0, 1, 0, 7),
    ("send", 2, -2, 2, 7),
    ("temporal", 1, -1, 1, 7),
    ("temporal", 0, -1, 1, 7),
    ("ring2", 0, 6, 0, 7),
    ("spatial", 0, -1, 1, 7),
    ("ring0", 0, 0, 0, 7),
    ("send", 1, -2, 2, 7),
    ("ring0", 1, 0, 0, 7),
    ("ring1", 1, 1, 0, 7),
    ("send", 0, -2, 2, 7),
    ("ring2", 1, 10, 0, 7),
)


def softmax_times(scores, values, factor):
    highest = jnp.max(scores, axis=-1, keepdims=True)
    weights = jnp.exp2((scores - highest) * factor)
    total = jnp.sum(weights, axis=-1, keepdims=True)
    mixed = jnp.dot(weights.astype(jnp.bfloat16), values, preferred_element_type=jnp.float32)
    return mixed / total


def scores_of(queries, keys):
    return lax.dot_general(queries, keys, (((1,), (1,)), ((), ())), preferred_element_type=jnp.float32)


def kernel(
    n_seq, n_head, chunks, kind_ref, qkv_hbm, weight_hbm, out,
    qkv, weight, packed, arrived, answers, returned, attended, partial, passing, order,
    qkv_sem, weight_sem, there_send, there_recv, back_send, back_recv, ring_send, ring_recv,
):
    heads, tokens, width = qkv.shape[1:]
    half = heads // 2
    groups = (half + 1) // 2
    dests = tokens // BLOCK // chunks
    stride = n_seq // dests
    share = tokens // n_head
    rows = share // chunks
    per_owner = rows // BLOCK
    side_columns = weight.shape[2] // 2
    columns = side_columns // STREAMS
    tiles = packed.shape[2]
    factor = width**-0.5 * math.log2(math.e)
    s = lax.axis_index("seq")
    g = lax.axis_index("head")
    side = (lax.rem(g + 1, n_head), lax.rem(g + n_head - 1, n_head))

    def wrapped(i, n):
        return jnp.where(i >= n, i - n, i)

    block = lax.div(s, stride)
    phase = lax.rem(s, stride)

    qkv_copy = pltpu.make_async_copy(qkv_hbm, qkv, qkv_sem)
    weight_copy = pltpu.make_async_copy(weight_hbm, weight, weight_sem)
    qkv_copy.start()

    barrier = pltpu.get_barrier_semaphore()

    def greet(i, _):
        pl.semaphore_signal(barrier, inc=1, device_id={"seq": wrapped(s + i, n_seq), "head": g}, device_id_type=MESH)
        return 0

    lax.fori_loop(1, n_seq, greet, 0)
    for y in side:
        pl.semaphore_signal(barrier, inc=1, device_id={"seq": s, "head": y}, device_id_type=MESH)

    found = [jnp.int32(0), jnp.int32(0)]
    listed = [jnp.int32(0)] * heads
    for i in range(heads):
        temporal = kind_ref[i] == 1
        place = jnp.where(temporal, found[1] + half, found[0])
        for j in range(heads):
            listed[j] = jnp.where(place == j, jnp.int32(i), listed[j])
        found[0] = found[0] + jnp.where(temporal, 0, 1)
        found[1] = found[1] + jnp.where(temporal, 1, 0)
    for j in range(heads):
        order[j] = listed[j]

    def tiles_of(q):
        return pl.ds(3 * q, min(3, tiles - 3 * q))

    def unit(kind, h):
        at = 6 * (h // 2) + 3 * (h % 2) + kind
        return at // 2, at % 2

    def pack(c, q):
        for o in range(n_head):
            of = pl.ds(pl.multiple_of(share * o + rows * c, rows), rows)
            found = {}
            for h in range(2 * q, min(2 * q + 2, half)):
                for kind in range(3):
                    found[unit(kind, h)] = (
                        qkv[kind, order[half + h], of, :].astype(jnp.float32).reshape(per_owner, BLOCK, width)
                    )
            for t in sorted({at[0] for at in found}):
                low = found[t, 0]
                both = jnp.concatenate([low, found.get((t, 1), low)], axis=1)
                packed[c, pl.ds(o * per_owner, per_owner), t] = both.astype(jnp.bfloat16)

    def part_of(tile, upper):
        half_tile = tile.astype(jnp.float32)[:, BLOCK * upper : BLOCK * (upper + 1)]
        return half_tile.reshape(half_tile.shape[0] * BLOCK, width).astype(jnp.bfloat16)

    def is_dest(c):
        return phase == lax.rem(c, stride)

    def send(c, q):
        pack(c, q)
        send_packed(c, q)

    def send_packed(c, q):
        slot = lax.div(c, stride)

        near, dst = lax.rem(c, stride), arrived.at[slot, s, tiles_of(q)]

        def remote(j):
            pltpu.make_async_remote_copy(
                src_ref=packed.at[c, j, tiles_of(q)], dst_ref=dst,
                send_sem=there_send.at[c, q], recv_sem=there_recv.at[slot, q],
                device_id={"seq": j * stride + near, "head": g}, device_id_type=MESH,
            ).start()

        @pl.when(is_dest(c))
        def _():
            pltpu.make_async_copy(packed.at[c, block, tiles_of(q)], dst, there_recv.at[slot, q]).start()

        @pl.when(jnp.logical_not(is_dest(c)))
        def _():
            remote(block)

        def one(i, _):
            remote(wrapped(block + i, dests))
            return 0

        lax.fori_loop(1, dests, one, 0, unroll=UNROLL)

    def temporal(c, q):
        slot = lax.div(c, stride)

        @pl.when(is_dest(c))
        def _():
            whole = arrived.at[slot, :, tiles_of(q)]
            pltpu.make_async_copy(whole, whole, there_recv.at[slot, q]).wait()
            n = n_seq * BLOCK
            same = lax.rem(lax.broadcasted_iota(jnp.int32, (n, n), 0), BLOCK) == lax.rem(
                lax.broadcasted_iota(jnp.int32, (n, n), 1), BLOCK
            )
            done = []
            for h in range(2 * q, min(2 * q + 2, half)):
                queries, keys, values = (
                    part_of(arrived[slot, :, unit(kind, h)[0]], unit(kind, h)[1]) for kind in range(3)
                )
                scores = jnp.where(same, scores_of(queries, keys), NEG)
                done.append(softmax_times(scores, values, factor).reshape(n_seq, BLOCK, width))
            answers[slot, q] = jnp.concatenate([done[0], done[-1]], axis=1).astype(jnp.bfloat16)

            dst = returned.at[c, q, block]
            pltpu.make_async_copy(answers.at[slot, q, s], dst, back_recv.at[c, q]).start()

            def one(i, _):
                to = wrapped(s + i, n_seq)
                pltpu.make_async_remote_copy(
                    src_ref=answers.at[slot, q, to], dst_ref=dst,
                    send_sem=back_send.at[slot, q], recv_sem=back_recv.at[c, q],
                    device_id={"seq": to, "head": g}, device_id_type=MESH,
                ).start()
                return 0

            lax.fori_loop(1, n_seq, one, 0, unroll=UNROLL)

    def spatial(c, _):
        slot = lax.rem(c, 2)
        for h in range(half):
            head = order[h]
            queries = jnp.concatenate(
                [qkv[0, head, pl.ds(pl.multiple_of(share * o + rows * c, rows), rows), :] for o in range(n_head)], axis=0
            )
            attended[slot, :, h * width : (h + 1) * width] = softmax_times(
                scores_of(queries, qkv[1, head]), qkv[2, head], factor
            ).astype(jnp.bfloat16)

    def ring_start(c, d, t, h):
        owner = lax.rem(g + (n_head - 1 if d == 0 else 1), n_head)
        pltpu.make_async_remote_copy(
            src_ref=partial.at[c, d, h, owner] if t == 0 else passing.at[c, d, h, t - 1],
            dst_ref=passing.at[c, d, h, t], send_sem=ring_send.at[c, d, h, t], recv_sem=ring_recv.at[c, d, h, t],
            device_id={"seq": s, "head": side[d]}, device_id_type=MESH,
        ).start()

    def ring_wait(c, d, t, h, sem):
        pltpu.make_async_copy(passing.at[c, d, h, t], passing.at[c, d, h, t], sem.at[c, d, h, t]).wait()

    def project(c, h):
        slot = lax.rem(c, 2)
        if h == 0:
            for q in range(groups):
                pltpu.make_async_copy(returned.at[c, q], returned.at[c, q], back_recv.at[c, q]).wait()
            for i in range(half):
                attended[slot, :, (half + i) * width : (half + i + 1) * width] = part_of(returned[c, i // 2], i % 2)
        step = 256 if columns % 256 == 0 else columns
        for d in range(2):
            for t in range(0, columns, step):
                cols = pl.ds(d * side_columns + h * columns + t, step)
                rows_of = jnp.concatenate([weight[order[i], :, cols] for i in range(heads)], axis=0)
                total = jnp.dot(attended[slot], rows_of, preferred_element_type=jnp.float32)
                partial[c, d, h, :, :, t : t + step] = total.astype(jnp.bfloat16).reshape(n_head, rows, step)
            ring_start(c, d, 0, h)

    def ring(t):
        def step(c, h):
            for d in range(2):
                ring_wait(c, d, t, h, ring_recv)
                owner = lax.rem(g + (2 * n_head - 2 - t if d == 0 else 2 + t), n_head)
                total = passing[c, d, h, t].astype(jnp.float32) + partial[c, d, h, owner].astype(jnp.float32)
                total = total.astype(jnp.bfloat16)
                if t < n_head - 2:
                    passing[c, d, h, t] = total
                    ring_start(c, d, t + 1, h)
                else:
                    first = d * side_columns + h * columns
                    out[pl.ds(pl.multiple_of(rows * c, rows), rows), first : first + columns] = total

        return step

    does = dict(send=send, send_packed=send_packed, temporal=temporal, spatial=spatial, project=project)
    for t in range(n_head - 1):
        does["ring%d" % t] = ring(t)
    lags = [entry[2] for entry in TICK]

    qkv_copy.wait()
    weight_copy.start()
    for q in range(groups):
        pack(jnp.int32(0), q)
    pl.semaphore_wait(barrier, n_seq - 1 + 2)
    for what, part, c in START:
        does[what](jnp.int32(c), part)
    weight_copy.wait()

    def tick(k, _):
        for what, part, lag, first, last in TICK:
            c = k - lag
            @pl.when(jnp.logical_and(c >= first, c <= last))
            def _(what=what, part=part, c=c):
                does[what](c, part)

        return 0

    lax.fori_loop(0, chunks + max(lags), tick, 0)

    def finish(c, _):
        slot = lax.div(c, stride)
        for h in range(STREAMS):
            for d in range(2):
                for t in range(n_head - 1):
                    ring_wait(c, d, t, h, ring_send)

        @pl.when(is_dest(c))
        def _():
            for q in range(groups):
                few = packed.at[c, pl.ds(0, dests - 1), tiles_of(q)]
                pltpu.make_async_copy(few, few, there_send.at[c, q]).wait()
                most = answers.at[slot, q, pl.ds(0, n_seq - 1)]
                pltpu.make_async_copy(most, most, back_send.at[slot, q]).wait()

        @pl.when(jnp.logical_not(is_dest(c)))
        def _():
            for q in range(groups):
                every = packed.at[c, :, tiles_of(q)]
                pltpu.make_async_copy(every, every, there_send.at[c, q]).wait()

        return 0

    lax.fori_loop(0, chunks, finish, 0)


def shards(n_seq, n_head, chunks, qkv, head_type, out_weight):
    kinds, tokens, heads, width = qkv.shape
    model = out_weight.shape[2]
    half = heads // 2
    groups, tiles = (half + 1) // 2, (3 * half + 1) // 2
    dests = tokens // BLOCK // chunks
    slots = chunks * dests // n_seq
    rows = tokens // n_head // chunks
    part = model // 2 // STREAMS
    bf16 = jnp.bfloat16
    dma = pltpu.SemaphoreType.DMA
    any_ = pl.BlockSpec(memory_space=pl.ANY)
    return pl.pallas_call(
        functools.partial(kernel, n_seq, n_head, chunks),
        out_shape=pltpu.VMEM((tokens // n_head, model), bf16),
        in_specs=[pl.BlockSpec(memory_space=pltpu.SMEM), any_, any_],
        out_specs=pl.BlockSpec(memory_space=pltpu.VMEM),
        scratch_shapes=[
            pltpu.VMEM((kinds, heads, tokens, width), bf16),
            pltpu.VMEM((heads, width, model), bf16),
            pltpu.VMEM((chunks, dests, tiles, 2 * BLOCK, width), bf16),
            pltpu.VMEM((slots, n_seq, tiles, 2 * BLOCK, width), bf16),
            pltpu.VMEM((slots, groups, n_seq, 2 * BLOCK, width), bf16),
            pltpu.VMEM((chunks, groups, dests, 2 * BLOCK, width), bf16),
            pltpu.VMEM((2, n_head * rows, heads * width), bf16),
            pltpu.VMEM((chunks, 2, STREAMS, n_head, rows, part), bf16),
            pltpu.VMEM((chunks, 2, STREAMS, n_head - 1, rows, part), bf16),
            pltpu.SMEM((heads,), jnp.int32),
            dma,
            dma,
            dma((chunks, groups)),
            dma((slots, groups)),
            dma((slots, groups)),
            dma((chunks, groups)),
            dma((chunks, 2, STREAMS, n_head - 1)),
            dma((chunks, 2, STREAMS, n_head - 1)),
        ],
        compiler_params=pltpu.CompilerParams(
            collective_id=0, has_side_effects=True, vmem_limit_bytes=56 * 1024 * 1024
        ),
        cost_estimate=pl.CostEstimate(flops=17_000_000_000, bytes_accessed=24_000_000, transcendentals=6_000_000),
    )(head_type, jnp.transpose(qkv, (0, 2, 1, 3)), out_weight)


def solution(mesh):
    n_seq, n_head = mesh.shape["seq"], mesh.shape["head"]
    return jax.shard_map(
        functools.partial(shards, n_seq, n_head, CHUNKS),
        mesh=mesh,
        in_specs=(P(None, "seq", "head", None), P("head"), P("head", None, None)),
        out_specs=P(("seq", "head"), None),
        check_vma=False,
    )
```

```python
import functools
import math

import jax
import jax.numpy as jnp
from jax import lax
from jax.experimental import pallas as pl
from jax.experimental.pallas import tpu as pltpu
from jax.sharding import PartitionSpec as P

MESH = pl.DeviceIdType.MESH
BLOCK = 8
CHUNKS = 8
UNROLL = 1
STREAMS = 2
NEG = -1e30
START = (
    ("send_packed", 2, 0),
    ("send_packed", 0, 0),
    ("send_packed", 1, 0),
    ("send", 2, 1),
    ("temporal", 2, 0),
    ("temporal", 0, 0),
    ("temporal", 1, 0),
    ("send", 0, 1),
    ("send", 1, 1),
    ("spatial", 0, 0),
)
TICK = (
    ("temporal", 2, -1, 1, 7),
    ("project", 0, 0, 0, 7),
    ("project", 1, 0, 0, 7),
    ("ring1", 0, 1, 0, 7),
    ("send", 2, -2, 2, 7),
    ("temporal", 1, -1, 1, 7),
    ("temporal", 0, -1, 1, 7),
    ("ring2", 0, 6, 0, 7),
    ("ring0", 0, 0, 0, 7),
    ("send", 1, -2, 2, 7),
    ("spatial", 0, -1, 1, 7),
    ("ring0", 1, 0, 0, 7),
    ("ring1", 1, 1, 0, 7),
    ("send", 0, -2, 2, 7),
    ("ring2", 1, 10, 0, 7),
)


def softmax_times(scores, values, factor):
    highest = jnp.max(scores, axis=-1, keepdims=True)
    weights = jnp.exp2((scores - highest) * factor)
    total = jnp.sum(weights, axis=-1, keepdims=True)
    mixed = jnp.dot(weights.astype(jnp.bfloat16), values, preferred_element_type=jnp.float32)
    return mixed / total


def scores_of(queries, keys):
    return lax.dot_general(queries, keys, (((1,), (1,)), ((), ())), preferred_element_type=jnp.float32)


def kernel(
    n_seq, n_head, chunks, kind_ref, qkv_hbm, weight_hbm, out,
    qkv, weight, packed, arrived, answers, returned, attended, partial, passing, order,
    qkv_sem, weight_sem, there_send, there_recv, back_send, back_recv, ring_send, ring_recv,
):
    heads, tokens, width = qkv.shape[1:]
    half = heads // 2
    groups = (half + 1) // 2
    dests = tokens // BLOCK // chunks
    stride = n_seq // dests
    share = tokens // n_head
    rows = share // chunks
    per_owner = rows // BLOCK
    side_columns = weight.shape[2] // 2
    columns = side_columns // STREAMS
    tiles = packed.shape[2]
    factor = width**-0.5 * math.log2(math.e)
    s = lax.axis_index("seq")
    g = lax.axis_index("head")
    side = (lax.rem(g + 1, n_head), lax.rem(g + n_head - 1, n_head))

    def wrapped(i, n):
        return jnp.where(i >= n, i - n, i)

    block = lax.div(s, stride)
    phase = lax.rem(s, stride)

    weight_copy = pltpu.make_async_copy(weight_hbm, weight, weight_sem)
    for kind in range(3):
        pltpu.make_async_copy(qkv_hbm.at[kind], qkv.at[kind], qkv_sem.at[kind]).start()

    barrier = pltpu.get_barrier_semaphore()

    def greet(i, _):
        pl.semaphore_signal(barrier, inc=1, device_id={"seq": wrapped(s + i, n_seq), "head": g}, device_id_type=MESH)
        return 0

    lax.fori_loop(1, n_seq, greet, 0)
    for y in side:
        pl.semaphore_signal(barrier, inc=1, device_id={"seq": s, "head": y}, device_id_type=MESH)

    found = [jnp.int32(0), jnp.int32(0)]
    listed = [jnp.int32(0)] * heads
    for i in range(heads):
        temporal = kind_ref[i] == 1
        place = jnp.where(temporal, found[1] + half, found[0])
        for j in range(heads):
            listed[j] = jnp.where(place == j, jnp.int32(i), listed[j])
        found[0] = found[0] + jnp.where(temporal, 0, 1)
        found[1] = found[1] + jnp.where(temporal, 1, 0)
    for j in range(heads):
        order[j] = listed[j]

    def tiles_of(q):
        return pl.ds(3 * q, min(3, tiles - 3 * q))

    def unit(kind, h):
        at = 6 * (h // 2) + 3 * (h % 2) + kind
        return at // 2, at % 2

    def pack(c, q):
        for o in range(n_head):
            of = pl.ds(pl.multiple_of(share * o + rows * c, rows), rows)
            found = {}
            for h in range(2 * q, min(2 * q + 2, half)):
                for kind in range(3):
                    found[unit(kind, h)] = (
                        qkv[kind, order[half + h], of, :].astype(jnp.float32).reshape(per_owner, BLOCK, width)
                    )
            for t in sorted({at[0] for at in found}):
                low = found[t, 0]
                both = jnp.concatenate([low, found.get((t, 1), low)], axis=1)
                packed[c, pl.ds(o * per_owner, per_owner), t] = both.astype(jnp.bfloat16)

    def part_of(tile, upper):
        half_tile = tile.astype(jnp.float32)[:, BLOCK * upper : BLOCK * (upper + 1)]
        return half_tile.reshape(half_tile.shape[0] * BLOCK, width).astype(jnp.bfloat16)

    def is_dest(c):
        return phase == lax.rem(c, stride)

    def send(c, q):
        pack(c, q)
        send_packed(c, q)

    def send_packed(c, q):
        slot = lax.div(c, stride)

        near, dst = lax.rem(c, stride), arrived.at[slot, s, tiles_of(q)]

        def remote(j):
            pltpu.make_async_remote_copy(
                src_ref=packed.at[c, j, tiles_of(q)], dst_ref=dst,
                send_sem=there_send.at[c, q], recv_sem=there_recv.at[slot, q],
                device_id={"seq": j * stride + near, "head": g}, device_id_type=MESH,
            ).start()

        @pl.when(is_dest(c))
        def _():
            pltpu.make_async_copy(packed.at[c, block, tiles_of(q)], dst, there_recv.at[slot, q]).start()

        @pl.when(jnp.logical_not(is_dest(c)))
        def _():
            remote(block)

        def one(i, _):
            remote(wrapped(block + i, dests))
            return 0

        lax.fori_loop(1, dests, one, 0, unroll=UNROLL)

    def temporal(c, q):
        slot = lax.div(c, stride)

        @pl.when(is_dest(c))
        def _():
            whole = arrived.at[slot, :, tiles_of(q)]
            pltpu.make_async_copy(whole, whole, there_recv.at[slot, q]).wait()
            n = n_seq * BLOCK
            same = lax.rem(lax.broadcasted_iota(jnp.int32, (n, n), 0), BLOCK) == lax.rem(
                lax.broadcasted_iota(jnp.int32, (n, n), 1), BLOCK
            )
            done = []
            for h in range(2 * q, min(2 * q + 2, half)):
                queries, keys, values = (
                    part_of(arrived[slot, :, unit(kind, h)[0]], unit(kind, h)[1]) for kind in range(3)
                )
                scores = jnp.where(same, scores_of(queries, keys), NEG)
                done.append(softmax_times(scores, values, factor).reshape(n_seq, BLOCK, width))
            answers[slot, q] = jnp.concatenate([done[0], done[-1]], axis=1).astype(jnp.bfloat16)

            dst = returned.at[c, q, block]
            pltpu.make_async_copy(answers.at[slot, q, s], dst, back_recv.at[c, q]).start()

            def one(i, _):
                to = wrapped(s + i, n_seq)
                pltpu.make_async_remote_copy(
                    src_ref=answers.at[slot, q, to], dst_ref=dst,
                    send_sem=back_send.at[slot, q], recv_sem=back_recv.at[c, q],
                    device_id={"seq": to, "head": g}, device_id_type=MESH,
                ).start()
                return 0

            lax.fori_loop(1, n_seq, one, 0, unroll=UNROLL)

    def spatial(c, _):
        slot = lax.rem(c, 2)
        for h in range(half):
            head = order[h]
            queries = jnp.concatenate(
                [qkv[0, head, pl.ds(pl.multiple_of(share * o + rows * c, rows), rows), :] for o in range(n_head)], axis=0
            )
            attended[slot, :, h * width : (h + 1) * width] = softmax_times(
                scores_of(queries, qkv[1, head]), qkv[2, head], factor
            ).astype(jnp.bfloat16)

    def ring_start(c, d, t, h):
        owner = lax.rem(g + (n_head - 1 if d == 0 else 1), n_head)
        pltpu.make_async_remote_copy(
            src_ref=partial.at[c, d, h, owner] if t == 0 else passing.at[c, d, h, t - 1],
            dst_ref=passing.at[c, d, h, t], send_sem=ring_send.at[c, d, h, t], recv_sem=ring_recv.at[c, d, h, t],
            device_id={"seq": s, "head": side[d]}, device_id_type=MESH,
        ).start()

    def ring_wait(c, d, t, h, sem):
        pltpu.make_async_copy(passing.at[c, d, h, t], passing.at[c, d, h, t], sem.at[c, d, h, t]).wait()

    def project(c, h):
        slot = lax.rem(c, 2)
        if h == 0:
            for q in range(groups):
                pltpu.make_async_copy(returned.at[c, q], returned.at[c, q], back_recv.at[c, q]).wait()
            for i in range(half):
                attended[slot, :, (half + i) * width : (half + i + 1) * width] = part_of(returned[c, i // 2], i % 2)
        step = 256 if columns % 256 == 0 else columns
        for d in range(2):
            for t in range(0, columns, step):
                cols = pl.ds(d * side_columns + h * columns + t, step)
                rows_of = jnp.concatenate([weight[order[i], :, cols] for i in range(heads)], axis=0)
                total = jnp.dot(attended[slot], rows_of, preferred_element_type=jnp.float32)
                partial[c, d, h, :, :, t : t + step] = total.astype(jnp.bfloat16).reshape(n_head, rows, step)
            ring_start(c, d, 0, h)

    def ring(t):
        def step(c, h):
            for d in range(2):
                ring_wait(c, d, t, h, ring_recv)
                owner = lax.rem(g + (2 * n_head - 2 - t if d == 0 else 2 + t), n_head)
                total = passing[c, d, h, t].astype(jnp.float32) + partial[c, d, h, owner].astype(jnp.float32)
                total = total.astype(jnp.bfloat16)
                if t < n_head - 2:
                    passing[c, d, h, t] = total
                    ring_start(c, d, t + 1, h)
                else:
                    first = d * side_columns + h * columns
                    out[pl.ds(pl.multiple_of(rows * c, rows), rows), first : first + columns] = total

        return step

    does = dict(send=send, send_packed=send_packed, temporal=temporal, spatial=spatial, project=project)
    for t in range(n_head - 1):
        does["ring%d" % t] = ring(t)
    lags = [entry[2] for entry in TICK]

    for kind in range(3):
        pltpu.make_async_copy(qkv_hbm.at[kind], qkv.at[kind], qkv_sem.at[kind]).wait()
    weight_copy.start()
    for q in range(groups):
        pack(jnp.int32(0), q)
    pl.semaphore_wait(barrier, n_seq - 1 + 2)
    for what, part, c in START:
        does[what](jnp.int32(c), part)
    weight_copy.wait()

    def tick(k, _):
        for what, part, lag, first, last in TICK:
            c = k - lag
            @pl.when(jnp.logical_and(c >= first, c <= last))
            def _(what=what, part=part, c=c):
                does[what](c, part)

        return 0

    lax.fori_loop(0, chunks + max(lags), tick, 0)

    def finish(c, _):
        slot = lax.div(c, stride)
        for h in range(STREAMS):
            for d in range(2):
                for t in range(n_head - 1):
                    ring_wait(c, d, t, h, ring_send)

        @pl.when(is_dest(c))
        def _():
            for q in range(groups):
                few = packed.at[c, pl.ds(0, dests - 1), tiles_of(q)]
                pltpu.make_async_copy(few, few, there_send.at[c, q]).wait()
                most = answers.at[slot, q, pl.ds(0, n_seq - 1)]
                pltpu.make_async_copy(most, most, back_send.at[slot, q]).wait()

        @pl.when(jnp.logical_not(is_dest(c)))
        def _():
            for q in range(groups):
                every = packed.at[c, :, tiles_of(q)]
                pltpu.make_async_copy(every, every, there_send.at[c, q]).wait()

        return 0

    lax.fori_loop(0, chunks, finish, 0)


def shards(n_seq, n_head, chunks, qkv, head_type, out_weight):
    kinds, tokens, heads, width = qkv.shape
    model = out_weight.shape[2]
    half = heads // 2
    groups, tiles = (half + 1) // 2, (3 * half + 1) // 2
    dests = tokens // BLOCK // chunks
    slots = chunks * dests // n_seq
    rows = tokens // n_head // chunks
    part = model // 2 // STREAMS
    bf16 = jnp.bfloat16
    dma = pltpu.SemaphoreType.DMA
    any_ = pl.BlockSpec(memory_space=pl.ANY)
    return pl.pallas_call(
        functools.partial(kernel, n_seq, n_head, chunks),
        out_shape=pltpu.VMEM((tokens // n_head, model), bf16),
        in_specs=[pl.BlockSpec(memory_space=pltpu.SMEM), any_, any_],
        out_specs=pl.BlockSpec(memory_space=pltpu.VMEM),
        scratch_shapes=[
            pltpu.VMEM((kinds, heads, tokens, width), bf16),
            pltpu.VMEM((heads, width, model), bf16),
            pltpu.VMEM((chunks, dests, tiles, 2 * BLOCK, width), bf16),
            pltpu.VMEM((slots, n_seq, tiles, 2 * BLOCK, width), bf16),
            pltpu.VMEM((slots, groups, n_seq, 2 * BLOCK, width), bf16),
            pltpu.VMEM((chunks, groups, dests, 2 * BLOCK, width), bf16),
            pltpu.VMEM((2, n_head * rows, heads * width), bf16),
            pltpu.VMEM((chunks, 2, STREAMS, n_head, rows, part), bf16),
            pltpu.VMEM((chunks, 2, STREAMS, n_head - 1, rows, part), bf16),
            pltpu.SMEM((heads,), jnp.int32),
            dma((3,)),
            dma,
            dma((chunks, groups)),
            dma((slots, groups)),
            dma((slots, groups)),
            dma((chunks, groups)),
            dma((chunks, 2, STREAMS, n_head - 1)),
            dma((chunks, 2, STREAMS, n_head - 1)),
        ],
        compiler_params=pltpu.CompilerParams(
            collective_id=0, has_side_effects=True, vmem_limit_bytes=56 * 1024 * 1024
        ),
        cost_estimate=pl.CostEstimate(flops=17_000_000_000, bytes_accessed=24_000_000, transcendentals=6_000_000),
    )(head_type, jnp.transpose(qkv, (0, 2, 1, 3)), out_weight)


def solution(mesh):
    n_seq, n_head = mesh.shape["seq"], mesh.shape["head"]
    return jax.shard_map(
        functools.partial(shards, n_seq, n_head, CHUNKS),
        mesh=mesh,
        in_specs=(P(None, "seq", "head", None), P("head"), P("head", None, None)),
        out_specs=P(("seq", "head"), None),
        check_vma=False,
    )
```

```python
import functools
import math

import jax
import jax.numpy as jnp
from jax import lax
from jax.experimental import pallas as pl
from jax.experimental.pallas import tpu as pltpu
from jax.sharding import PartitionSpec as P

MESH = pl.DeviceIdType.MESH
BLOCK = 8
CHUNKS = 8
UNROLL = 1
STREAMS = 2
NEG = -1e30
START = (
    ("send_packed", 2, 0),
    ("send_packed", 0, 0),
    ("send_packed", 1, 0),
    ("send", 2, 1),
    ("temporal", 2, 0),
    ("temporal", 0, 0),
    ("temporal", 1, 0),
    ("send", 0, 1),
    ("spatial", 0, 0),
    ("send", 1, 1),
)
TICK = (
    ("temporal", 2, -1, 1, 7),
    ("project", 0, 0, 0, 7),
    ("project", 1, 0, 0, 7),
    ("ring1", 0, 1, 0, 7),
    ("send", 2, -2, 2, 7),
    ("temporal", 1, -1, 1, 7),
    ("temporal", 0, -1, 1, 7),
    ("ring2", 0, 6, 0, 7),
    ("ring0", 0, 0, 0, 7),
    ("send", 1, -2, 2, 7),
    ("spatial", 0, -1, 1, 7),
    ("ring0", 1, 0, 0, 7),
    ("ring1", 1, 1, 0, 7),
    ("send", 0, -2, 2, 7),
    ("ring2", 1, 10, 0, 7),
)


def softmax_times(scores, values, factor):
    highest = jnp.max(scores, axis=-1, keepdims=True)
    weights = jnp.exp2((scores - highest) * factor)
    total = jnp.sum(weights, axis=-1, keepdims=True)
    mixed = jnp.dot(weights.astype(jnp.bfloat16), values, preferred_element_type=jnp.float32)
    return mixed / total


def scores_of(queries, keys):
    return lax.dot_general(queries, keys, (((1,), (1,)), ((), ())), preferred_element_type=jnp.float32)


def kernel(
    n_seq, n_head, chunks, kind_ref, qkv_hbm, weight_hbm, out,
    qkv, weight, packed, arrived, answers, returned, attended, partial, passing, order,
    qkv_sem, weight_sem, there_send, there_recv, back_send, back_recv, ring_send, ring_recv,
):
    heads, tokens, width = qkv.shape[1:]
    half = heads // 2
    groups = (half + 1) // 2
    dests = tokens // BLOCK // chunks
    stride = n_seq // dests
    share = tokens // n_head
    rows = share // chunks
    per_owner = rows // BLOCK
    side_columns = weight.shape[2] // 2
    columns = side_columns // STREAMS
    tiles = packed.shape[2]
    factor = width**-0.5 * math.log2(math.e)
    s = lax.axis_index("seq")
    g = lax.axis_index("head")
    side = (lax.rem(g + 1, n_head), lax.rem(g + n_head - 1, n_head))

    def wrapped(i, n):
        return jnp.where(i >= n, i - n, i)

    block = lax.div(s, stride)
    phase = lax.rem(s, stride)

    weight_copy = pltpu.make_async_copy(weight_hbm, weight, weight_sem)
    for kind in range(3):
        pltpu.make_async_copy(qkv_hbm.at[kind], qkv.at[kind], qkv_sem.at[kind]).start()

    barrier = pltpu.get_barrier_semaphore()

    def greet(i, _):
        pl.semaphore_signal(barrier, inc=1, device_id={"seq": wrapped(s + i, n_seq), "head": g}, device_id_type=MESH)
        return 0

    lax.fori_loop(1, n_seq, greet, 0)
    for y in side:
        pl.semaphore_signal(barrier, inc=1, device_id={"seq": s, "head": y}, device_id_type=MESH)

    found = [jnp.int32(0), jnp.int32(0)]
    listed = [jnp.int32(0)] * heads
    for i in range(heads):
        temporal = kind_ref[i] == 1
        place = jnp.where(temporal, found[1] + half, found[0])
        for j in range(heads):
            listed[j] = jnp.where(place == j, jnp.int32(i), listed[j])
        found[0] = found[0] + jnp.where(temporal, 0, 1)
        found[1] = found[1] + jnp.where(temporal, 1, 0)
    for j in range(heads):
        order[j] = listed[j]

    def tiles_of(q):
        return pl.ds(3 * q, min(3, tiles - 3 * q))

    def unit(kind, h):
        at = 6 * (h // 2) + 3 * (h % 2) + kind
        return at // 2, at % 2

    def pack(c, q):
        for o in range(n_head):
            of = pl.ds(pl.multiple_of(share * o + rows * c, rows), rows)
            found = {}
            for h in range(2 * q, min(2 * q + 2, half)):
                for kind in range(3):
                    found[unit(kind, h)] = (
                        qkv[kind, order[half + h], of, :].astype(jnp.float32).reshape(per_owner, BLOCK, width)
                    )
            for t in sorted({at[0] for at in found}):
                low = found[t, 0]
                both = jnp.concatenate([low, found.get((t, 1), low)], axis=1)
                packed[c, pl.ds(o * per_owner, per_owner), t] = both.astype(jnp.bfloat16)

    def part_of(tile, upper):
        half_tile = tile.astype(jnp.float32)[:, BLOCK * upper : BLOCK * (upper + 1)]
        return half_tile.reshape(half_tile.shape[0] * BLOCK, width).astype(jnp.bfloat16)

    def is_dest(c):
        return phase == lax.rem(c, stride)

    def send(c, q):
        pack(c, q)
        send_packed(c, q)

    def send_packed(c, q):
        slot = lax.div(c, stride)

        near, dst = lax.rem(c, stride), arrived.at[slot, s, tiles_of(q)]

        def remote(j):
            pltpu.make_async_remote_copy(
                src_ref=packed.at[c, j, tiles_of(q)], dst_ref=dst,
                send_sem=there_send.at[c, q], recv_sem=there_recv.at[slot, q],
                device_id={"seq": j * stride + near, "head": g}, device_id_type=MESH,
            ).start()

        @pl.when(is_dest(c))
        def _():
            pltpu.make_async_copy(packed.at[c, block, tiles_of(q)], dst, there_recv.at[slot, q]).start()

        @pl.when(jnp.logical_not(is_dest(c)))
        def _():
            remote(block)

        def one(i, _):
            remote(wrapped(block + i, dests))
            return 0

        lax.fori_loop(1, dests, one, 0, unroll=UNROLL)

    def temporal(c, q):
        slot = lax.div(c, stride)

        @pl.when(is_dest(c))
        def _():
            whole = arrived.at[slot, :, tiles_of(q)]
            pltpu.make_async_copy(whole, whole, there_recv.at[slot, q]).wait()
            n = n_seq * BLOCK
            same = lax.rem(lax.broadcasted_iota(jnp.int32, (n, n), 0), BLOCK) == lax.rem(
                lax.broadcasted_iota(jnp.int32, (n, n), 1), BLOCK
            )
            done = []
            for h in range(2 * q, min(2 * q + 2, half)):
                queries, keys, values = (
                    part_of(arrived[slot, :, unit(kind, h)[0]], unit(kind, h)[1]) for kind in range(3)
                )
                scores = jnp.where(same, scores_of(queries, keys), NEG)
                done.append(softmax_times(scores, values, factor).reshape(n_seq, BLOCK, width))
            answers[slot, q] = jnp.concatenate([done[0], done[-1]], axis=1).astype(jnp.bfloat16)

            dst = returned.at[c, q, block]
            pltpu.make_async_copy(answers.at[slot, q, s], dst, back_recv.at[c, q]).start()

            def one(i, _):
                to = wrapped(s + i, n_seq)
                pltpu.make_async_remote_copy(
                    src_ref=answers.at[slot, q, to], dst_ref=dst,
                    send_sem=back_send.at[slot, q], recv_sem=back_recv.at[c, q],
                    device_id={"seq": to, "head": g}, device_id_type=MESH,
                ).start()
                return 0

            lax.fori_loop(1, n_seq, one, 0, unroll=UNROLL)

    def spatial(c, _):
        slot = lax.rem(c, 2)
        for h in range(half):
            head = order[h]
            queries = jnp.concatenate(
                [qkv[0, head, pl.ds(pl.multiple_of(share * o + rows * c, rows), rows), :] for o in range(n_head)], axis=0
            )
            attended[slot, :, h * width : (h + 1) * width] = softmax_times(
                scores_of(queries, qkv[1, head]), qkv[2, head], factor
            ).astype(jnp.bfloat16)

    def ring_start(c, d, t, h):
        owner = lax.rem(g + (n_head - 1 if d == 0 else 1), n_head)
        pltpu.make_async_remote_copy(
            src_ref=partial.at[c, d, h, owner] if t == 0 else passing.at[c, d, h, t - 1],
            dst_ref=passing.at[c, d, h, t], send_sem=ring_send.at[c, d, h, t], recv_sem=ring_recv.at[c, d, h, t],
            device_id={"seq": s, "head": side[d]}, device_id_type=MESH,
        ).start()

    def ring_wait(c, d, t, h, sem):
        pltpu.make_async_copy(passing.at[c, d, h, t], passing.at[c, d, h, t], sem.at[c, d, h, t]).wait()

    def project(c, h):
        slot = lax.rem(c, 2)
        if h == 0:
            for q in range(groups):
                pltpu.make_async_copy(returned.at[c, q], returned.at[c, q], back_recv.at[c, q]).wait()
            for i in range(half):
                attended[slot, :, (half + i) * width : (half + i + 1) * width] = part_of(returned[c, i // 2], i % 2)
        step = 640 if columns % 640 == 0 else columns
        for d in range(2):
            for t in range(0, columns, step):
                cols = pl.ds(d * side_columns + h * columns + t, step)
                rows_of = jnp.concatenate([weight[order[i], :, cols] for i in range(heads)], axis=0)
                total = jnp.dot(attended[slot], rows_of, preferred_element_type=jnp.float32)
                partial[c, d, h, :, :, t : t + step] = total.astype(jnp.bfloat16).reshape(n_head, rows, step)
            ring_start(c, d, 0, h)

    def ring(t):
        def step(c, h):
            for d in range(2):
                ring_wait(c, d, t, h, ring_recv)
                owner = lax.rem(g + (2 * n_head - 2 - t if d == 0 else 2 + t), n_head)
                total = passing[c, d, h, t].astype(jnp.float32) + partial[c, d, h, owner].astype(jnp.float32)
                total = total.astype(jnp.bfloat16)
                if t < n_head - 2:
                    passing[c, d, h, t] = total
                    ring_start(c, d, t + 1, h)
                else:
                    first = d * side_columns + h * columns
                    out[pl.ds(pl.multiple_of(rows * c, rows), rows), first : first + columns] = total

        return step

    does = dict(send=send, send_packed=send_packed, temporal=temporal, spatial=spatial, project=project)
    for t in range(n_head - 1):
        does["ring%d" % t] = ring(t)
    lags = [entry[2] for entry in TICK]

    for kind in range(3):
        pltpu.make_async_copy(qkv_hbm.at[kind], qkv.at[kind], qkv_sem.at[kind]).wait()
    weight_copy.start()
    for q in range(groups):
        pack(jnp.int32(0), q)
    pl.semaphore_wait(barrier, n_seq - 1 + 2)
    for what, part, c in START:
        does[what](jnp.int32(c), part)
    weight_copy.wait()

    def tick(k, _):
        for what, part, lag, first, last in TICK:
            c = k - lag
            @pl.when(jnp.logical_and(c >= first, c <= last))
            def _(what=what, part=part, c=c):
                does[what](c, part)

        return 0

    lax.fori_loop(0, chunks + max(lags), tick, 0)

    def finish(c, _):
        slot = lax.div(c, stride)
        for h in range(STREAMS):
            for d in range(2):
                for t in range(n_head - 1):
                    ring_wait(c, d, t, h, ring_send)

        @pl.when(is_dest(c))
        def _():
            for q in range(groups):
                few = packed.at[c, pl.ds(0, dests - 1), tiles_of(q)]
                pltpu.make_async_copy(few, few, there_send.at[c, q]).wait()
                most = answers.at[slot, q, pl.ds(0, n_seq - 1)]
                pltpu.make_async_copy(most, most, back_send.at[slot, q]).wait()

        @pl.when(jnp.logical_not(is_dest(c)))
        def _():
            for q in range(groups):
                every = packed.at[c, :, tiles_of(q)]
                pltpu.make_async_copy(every, every, there_send.at[c, q]).wait()

        return 0

    lax.fori_loop(0, chunks, finish, 0)


def shards(n_seq, n_head, chunks, qkv, head_type, out_weight):
    kinds, tokens, heads, width = qkv.shape
    model = out_weight.shape[2]
    half = heads // 2
    groups, tiles = (half + 1) // 2, (3 * half + 1) // 2
    dests = tokens // BLOCK // chunks
    slots = chunks * dests // n_seq
    rows = tokens // n_head // chunks
    part = model // 2 // STREAMS
    bf16 = jnp.bfloat16
    dma = pltpu.SemaphoreType.DMA
    any_ = pl.BlockSpec(memory_space=pl.ANY)
    return pl.pallas_call(
        functools.partial(kernel, n_seq, n_head, chunks),
        out_shape=pltpu.VMEM((tokens // n_head, model), bf16),
        in_specs=[pl.BlockSpec(memory_space=pltpu.SMEM), any_, any_],
        out_specs=pl.BlockSpec(memory_space=pltpu.VMEM),
        scratch_shapes=[
            pltpu.VMEM((kinds, heads, tokens, width), bf16),
            pltpu.VMEM((heads, width, model), bf16),
            pltpu.VMEM((chunks, dests, tiles, 2 * BLOCK, width), bf16),
            pltpu.VMEM((slots, n_seq, tiles, 2 * BLOCK, width), bf16),
            pltpu.VMEM((slots, groups, n_seq, 2 * BLOCK, width), bf16),
            pltpu.VMEM((chunks, groups, dests, 2 * BLOCK, width), bf16),
            pltpu.VMEM((2, n_head * rows, heads * width), bf16),
            pltpu.VMEM((chunks, 2, STREAMS, n_head, rows, part), bf16),
            pltpu.VMEM((chunks, 2, STREAMS, n_head - 1, rows, part), bf16),
            pltpu.SMEM((heads,), jnp.int32),
            dma((3,)),
            dma,
            dma((chunks, groups)),
            dma((slots, groups)),
            dma((slots, groups)),
            dma((chunks, groups)),
            dma((chunks, 2, STREAMS, n_head - 1)),
            dma((chunks, 2, STREAMS, n_head - 1)),
        ],
        compiler_params=pltpu.CompilerParams(
            collective_id=0, has_side_effects=True, vmem_limit_bytes=56 * 1024 * 1024
        ),
        cost_estimate=pl.CostEstimate(flops=17_000_000_000, bytes_accessed=24_000_000, transcendentals=6_000_000),
    )(head_type, jnp.transpose(qkv, (0, 2, 1, 3)), out_weight)


def solution(mesh):
    n_seq, n_head = mesh.shape["seq"], mesh.shape["head"]
    return jax.shard_map(
        functools.partial(shards, n_seq, n_head, CHUNKS),
        mesh=mesh,
        in_specs=(P(None, "seq", "head", None), P("head"), P("head", None, None)),
        out_specs=P(("seq", "head"), None),
        check_vma=False,
    )
```
